1024 devices in a mesh: dp: 16 (over x, core), shard: 64 (over z, y).
Axes of the slice: x: 8, y: 8, z: 8, core: 2. Of those that a mesh axis runs over, the one named last changes fastest.
Arguments:
- momentum: float32 [4096, 7168], P('dp', 'shard'), may hold values from -6 to 6
- gradient: bfloat16 [4096, 7168], P('dp', 'shard'), may hold values from -120 to 120
Outputs:
- new_momentum: float32 [4096, 7168], P('dp', 'shard')
- update: float32 [4096, 7168], P('dp', 'shard')
The draws below stay inside these ranges and needn't reach their ends.
All inputs are finite; a program needn't handle non-finite values.
Results may differ from the reference program's by a relative error of at most 0.0038.
The reference program's roundings to bfloat16 on the way count: a program that leaves them out, or rounds other values in their place, can miss the bound.
Values may be sent and summed in bfloat16 or wider, within the bound.
A program may use at most 32 MiB of HBM per device.

```python
import math
import jax
import jax.numpy as jnp
from jax import lax

D = 7168
STEPS = 2
ROWS = 4096


def draw_gradient(key, part):
    first_key, second_key, third_key = jax.random.split(jax.random.fold_in(key, 7), 3)
    trend = jnp.exp(jnp.arange(ROWS, dtype=jnp.float32) / ROWS * math.log(3.0))
    row_scale = trend * jnp.exp(jax.random.uniform(second_key, (ROWS,), jnp.float32, 0.0, math.log(10.0)))
    column_scale = jnp.exp(jax.random.uniform(third_key, (D,), jnp.float32, 0.0, math.log(10.0)))
    noise = jnp.clip(jax.random.normal(first_key, (ROWS, D), jnp.float32), -4.0, 4.0)
    values = noise * row_scale[:, None] * column_scale[None, :] / 10.0
    return values.astype(jnp.bfloat16)


def level_of(rng, extent, shards, smallest, largest):
    factor_of, own = 1.0, jax.random.fold_in(rng, 6)
    for position, shards_of in shards:
        steps = jnp.exp(jax.random.uniform(jax.random.fold_in(own, position), (shards_of,), jnp.float32, smallest / len(shards), largest / len(shards)))
        factor_of = factor_of * jnp.repeat(steps, extent[position] // shards_of).reshape([-1 if axis == position else 1 for axis in range(len(extent))])
    return factor_of


def normal_values(key, dims, scale, limit, cuts=(), held_as=jnp.bfloat16):
    loudness = level_of(key, dims, cuts, -0.22, 0.18) if cuts else 1.0
    drawn = jax.random.normal(key, dims, jnp.float32) * scale * loudness
    return jnp.minimum(jnp.maximum(drawn, -limit), limit).astype(held_as)


def setup_inputs(seed: int = 0) -> dict:
    key_list = jax.random.split(jax.random.key(seed), 3)
    momentum = normal_values(key_list[0], (ROWS, D), 1.0, 6.0, ((0, 16), (1, 64)), jnp.float32)
    gradient = draw_gradient(jax.random.fold_in(key_list[2], 71), 0)
    return dict(momentum=momentum, gradient=gradient)


momentum_decay = 0.95
linear_term = 3.4445
cubic_term = -4.775
quintic_term = 2.0315

def reference(momentum, gradient):
    grad_full = gradient.astype(jnp.float32)
    new_momentum = momentum_decay * momentum + grad_full
    current = grad_full + momentum_decay * new_momentum
    for iteration in range(STEPS):
        matrix = current.astype(jnp.bfloat16)
        gram_matrix = jnp.dot(matrix, matrix.T, preferred_element_type=jnp.float32).astype(jnp.bfloat16)
        square_sum = jnp.sum(jnp.square(gram_matrix.astype(jnp.float32)))
        inverse_norm = lax.rsqrt(square_sum)
        root_scale = jnp.sqrt(inverse_norm)
        first_product = jnp.dot(gram_matrix, matrix, preferred_element_type=jnp.float32)
        mixture = (cubic_term * root_scale * matrix.astype(jnp.float32) + quintic_term * root_scale * inverse_norm * first_product).astype(jnp.bfloat16)
        second_product = jnp.dot(gram_matrix, mixture, preferred_element_type=jnp.float32)
        current = linear_term * root_scale * matrix.astype(jnp.float32) + inverse_norm * second_product
    update = math.sqrt(D) * current
    return (new_momentum, update)
```

```python
import math

import jax
import jax.numpy as jnp
from jax import lax
from jax.experimental import pallas as pl
from jax.experimental.pallas import tpu as pltpu
from jax.sharding import Mesh
from jax.sharding import PartitionSpec as P

D = 7168
STEPS = 2
MESH = pl.DeviceIdType.MESH

momentum_decay = 0.95
linear_term = 3.4445
cubic_term = -4.775
quintic_term = 2.0315

SUM_TYPE = jnp.float32


def dot(a, b, dims=(1, 0)):
    return lax.dot_general(a, b, (((dims[0],), (dims[1],)), ((), ())), preferred_element_type=jnp.float32)


def kernel(sizes, start_ref, update_ref, panel, mixed, gram, big_out, big_in, held, small_out, small_in, squares, send_sem, recv_sem):
    nx, nz, ny = sizes
    half_of = (("z", nz), ("y", ny))
    x, core, z, y = (lax.axis_index(a) for a in ("x", "core", "z", "y"))
    place = {"x": x, "z": z, "y": y}
    dp = 2 * x + core
    sign = 1 - 2 * core
    rows = gram.shape[-1]

    def around(p, n):
        return lax.rem(p + 2 * n, n)

    def to(axis, n, step):
        return {axis: around(place[axis] + step, n)}

    barrier = pltpu.get_barrier_semaphore()
    for axis, n in half_of:
        for step in (1, -1):
            pl.semaphore_signal(barrier, inc=1, device_id=to(axis, n, step), device_id_type=MESH)
    for k in range(1, 2 * nx):
        other = lax.rem(dp + k, 2 * nx)
        pl.semaphore_signal(barrier, inc=1, device_id={"x": other // 2, "core": other % 2}, device_id_type=MESH)
    pl.semaphore_wait(barrier, 4 + 2 * nx - 1)

    sent = []

    def send(src, dst, device):
        k = len(sent)
        copy = pltpu.make_async_remote_copy(
            src_ref=src, dst_ref=dst, send_sem=send_sem.at[k], recv_sem=recv_sem.at[k], device_id=device, device_id_type=MESH
        )
        copy.start()
        sent.append(copy)
        return copy

    def ring_gather(axis, n, at, then):
        p = place[axis]
        ways = [[sign, n // 2, None], [-sign, (n - 1) // 2, None]]
        for t in range(n // 2 + 1):
            for way in ways:
                s, count, copy = way
                if t > count:
                    continue
                owner = around(p - s * t, n)
                if t > 0:
                    copy.wait_recv()
                if t < count:
                    way[2] = send(at(owner), at(owner), to(axis, n, s))
                if t > 0:
                    then(owner)
            yield

    def ring_sum(axis, n, local, out, into, add_type):
        p = place[axis]
        ways = [[sign, n // 2, None, 0], [-sign, (n - 1) // 2, None, n // 2]]
        for t in range(n // 2):
            for way in ways:
                s, count, copy, base = way
                if t >= count:
                    continue
                q = around(p + s * (count - t), n)
                value = local(q)
                if t > 0:
                    copy.wait_recv()
                    value = value + into[base + t - 1].astype(jnp.float32)
                out[base + t] = value.astype(add_type)
                way[2] = send(out.at[base + t], into.at[base + t], to(axis, n, s))
            yield
        value = local(p)
        for s, count, copy, base in ways:
            if count:
                copy.wait_recv()
                value = value + into[base + count - 1].astype(jnp.float32)
        yield value

    def together(*parts):
        last = [None] * len(parts)
        live = list(range(len(parts)))
        while live:
            for k in list(live):
                try:
                    last[k] = next(parts[k])
                except StopIteration:
                    live.remove(k)
        return last

    def gather_dp(buf):
        sibling = []

        def pass_on(owner):
            b = 2 * owner + core
            sibling.append(send(buf.at[b], buf.at[b], {"core": 1 - core}))

        ring = ring_gather("x", nx, lambda o: buf.at[2 * o + core], pass_on)
        next(ring)
        pass_on(x)
        together(ring)
        for copy in sibling:
            copy.wait_recv()

    current = start_ref[...]
    for it in range(STEPS):
        matrix = current.astype(jnp.bfloat16)
        wide, mix, g = panel.at[it], mixed.at[it], gram.at[it]
        wide[dp] = matrix
        gather_dp(wide)

        def local_of(first):
            return lambda q: dot(wide[first + q], wide[dp], (0, 0))

        sums = together(
            *(
                ring_sum(axis, n, local_of(h * nz), big_out.at[it, h], big_in.at[it, h], big_out.dtype)
                for h, (axis, n) in enumerate(half_of)
            )
        )
        part = rows // nz
        for h in range(2):
            held[h] = sums[h]

        def part_of(h):
            return lambda q: held[h, pl.ds(pl.multiple_of(q * part, part), part), :]

        crossed = (half_of[1], half_of[0])
        tiles = together(
            *(
                ring_sum(axis, n, part_of(h), small_out.at[it, h], small_in.at[it, h], small_out.dtype)
                for h, (axis, n) in enumerate(crossed)
            )
        )
        own = (z, nz + y)

        def tile_of(h):
            return lambda q: g.at[own[h], pl.ds(pl.multiple_of(q * part, part), part), :]

        for h, (axis, n) in enumerate(crossed):
            tile_of(h)(place[axis])[...] = tiles[h].astype(jnp.bfloat16)
        together(*(ring_gather(axis, n, tile_of(h), lambda o: None) for h, (axis, n) in enumerate(crossed)))

        square, first = [], []

        def use(block):
            value = g[block]
            v = value.astype(jnp.float32)
            v = (v * v).reshape(rows // 8, 8, rows).sum(axis=0)
            square.append(v[:, : rows // 2] + v[:, rows // 2 :])
            first.append(dot(wide[block], value))
            if len(first) > 1:
                square[:] = [square[0] + square[1]]
                first[:] = [first[0] + first[1]]

        rings = [
            ring_gather(axis, n, lambda o, h=h: g.at[h * nz + o], lambda o, h=h: use(h * nz + o))
            for h, (axis, n) in enumerate(half_of)
        ]
        for ring in rings:
            next(ring)
        use(own[0])
        use(own[1])
        together(*rings)

        squares[it, dp] = square[0]
        told = []
        for k in range(1, 2 * nx):
            other = lax.rem(dp + k, 2 * nx)
            told.append(send(squares.at[it, dp], squares.at[it, dp], {"x": other // 2, "core": other % 2}))
        for copy in told:
            copy.wait_recv()
        total = jnp.sum(squares[it], axis=0)
        total = jnp.sum(jnp.sum(total, axis=1, keepdims=True), axis=0, keepdims=True)
        inverse_norm = lax.rsqrt(total)
        root_scale = jnp.sqrt(inverse_norm)
        matrix_full = matrix.astype(jnp.float32)
        mix[dp] = (
            cubic_term * root_scale * matrix_full + quintic_term * root_scale * inverse_norm * first[0]
        ).astype(jnp.bfloat16)
        gather_dp(mix)
        second = dot(mix[0], g[0])
        for j in range(1, 2 * nx):
            second = second + dot(mix[j], g[j])
        current = linear_term * root_scale * matrix_full + inverse_norm * second
    update_ref[...] = math.sqrt(D) * current
    for copy in sent:
        copy.wait_send()


def body(sizes, momentum, gradient):
    nx, nz, ny = sizes
    grad_full = gradient.T.astype(jnp.float32)
    new_momentum = momentum_decay * momentum.T + grad_full
    current = grad_full + momentum_decay * new_momentum
    columns, rows = current.shape
    part = rows // nz
    copies = STEPS * 110
    update = pl.pallas_call(
        lambda *refs: kernel(sizes, *refs),
        out_shape=jax.ShapeDtypeStruct((columns, rows), jnp.float32),
        in_specs=[pl.BlockSpec(memory_space=pltpu.VMEM)],
        out_specs=pl.BlockSpec(memory_space=pltpu.VMEM),
        scratch_shapes=[
            pltpu.VMEM((STEPS, 2 * nx, columns, rows), jnp.bfloat16),
            pltpu.VMEM((STEPS, 2 * nx, columns, rows), jnp.bfloat16),
            pltpu.VMEM((STEPS, nz + ny, rows, rows), jnp.bfloat16),
            pltpu.VMEM((STEPS, 2, nz - 1, rows, rows), SUM_TYPE),
            pltpu.VMEM((STEPS, 2, nz - 1, rows, rows), SUM_TYPE),
            pltpu.VMEM((2, rows, rows), jnp.float32),
            pltpu.VMEM((STEPS, 2, nz - 1, part, rows), jnp.float32),
            pltpu.VMEM((STEPS, 2, nz - 1, part, rows), jnp.float32),
            pltpu.VMEM((STEPS, 2 * nx, 8, rows // 2), jnp.float32),
            pltpu.SemaphoreType.DMA((copies,)),
            pltpu.SemaphoreType.DMA((copies,)),
        ],
        compiler_params=pltpu.CompilerParams(collective_id=0, has_side_effects=True, vmem_limit_bytes=52 * 2**20),
    )(current)
    return new_momentum.T, update.T


def solution(mesh):
    split = Mesh(mesh.devices.reshape(8, 2, 8, 8), ("x", "core", "z", "y"))
    spec = P(("x", "core"), ("z", "y"))
    return jax.shard_map(
        lambda m, g: body((8, 8, 8), m, g),
        mesh=split,
        in_specs=(spec, spec),
        out_specs=(spec, spec),
        check_vma=False,
    )
```

```python
import math

import jax
import jax.numpy as jnp
from jax import lax
from jax.experimental import pallas as pl
from jax.experimental.pallas import tpu as pltpu
from jax.sharding import Mesh
from jax.sharding import PartitionSpec as P

D = 7168
STEPS = 2
MESH = pl.DeviceIdType.MESH

momentum_decay = 0.95
linear_term = 3.4445
cubic_term = -4.775
quintic_term = 2.0315

SUM_TYPE = jnp.bfloat16
SMALL = jnp.bfloat16
SUBS = 2


def dot(a, b, dims=(1, 0)):
    return lax.dot_general(a, b, (((dims[0],), (dims[1],)), ((), ())), preferred_element_type=jnp.float32)


def kernel(sizes, start_ref, update_ref, panel, mixed, gram, big_out, big_in, held, small_out, small_in, squares, send_sem, recv_sem):
    nx, nz, ny = sizes
    half_of = (("z", nz), ("y", ny))
    x, core, z, y = (lax.axis_index(a) for a in ("x", "core", "z", "y"))
    place = {"x": x, "z": z, "y": y}
    dp = 2 * x + core
    sign = 1 - 2 * core
    rows = gram.shape[-1]

    def around(p, n):
        return lax.rem(p + 2 * n, n)

    def to(axis, n, step):
        return {axis: around(place[axis] + step, n)}

    barrier = pltpu.get_barrier_semaphore()
    for axis, n in half_of:
        for step in range(1, n):
            pl.semaphore_signal(barrier, inc=1, device_id=to(axis, n, step), device_id_type=MESH)
    for k in range(1, 2 * nx):
        other = lax.rem(dp + k, 2 * nx)
        pl.semaphore_signal(barrier, inc=1, device_id={"x": other // 2, "core": other % 2}, device_id_type=MESH)
    pl.semaphore_wait(barrier, nz + ny + 2 * nx - 3)

    sent = []

    def send(src, dst, device):
        k = len(sent)
        copy = pltpu.make_async_remote_copy(
            src_ref=src, dst_ref=dst, send_sem=send_sem.at[k], recv_sem=recv_sem.at[k], device_id=device, device_id_type=MESH
        )
        copy.start()
        sent.append(copy)
        return copy

    def ring_gather(axis, n, at, then):
        p = place[axis]
        ways = [[sign, n // 2, None], [-sign, (n - 1) // 2, None]]
        for t in range(n // 2 + 1):
            for way in ways:
                s, count, copy = way
                if t > count:
                    continue
                owner = around(p - s * t, n)
                if t > 0:
                    copy.wait_recv()
                if t < count:
                    way[2] = send(at(owner), at(owner), to(axis, n, s))
                if t > 0:
                    then(owner)
            yield

    def ring_sum(axis, n, local, out, into, add_type):
        p = place[axis]
        ways = [[sign, n // 2, None, 0], [-sign, (n - 1) // 2, None, n // 2]]
        for t in range(n // 2):
            for way in ways:
                s, count, copy, base = way
                if t >= count:
                    continue
                q = around(p + s * (count - t), n)
                value = local(q)
                if t > 0:
                    copy.wait_recv()
                    value = value + into[base + t - 1].astype(jnp.float32)
                out[base + t] = value.astype(add_type)
                way[2] = send(out.at[base + t], into.at[base + t], to(axis, n, s))
            yield
        value = local(p)
        for s, count, copy, base in ways:
            if count:
                copy.wait_recv()
                value = value + into[base + count - 1].astype(jnp.float32)
        yield value

    def far_first(n):
        return sorted(range(1, n), key=lambda k: -min(k, n - k))

    def direct_gather(axis, n, at):
        own = at(place[axis])
        return [send(own, own, to(axis, n, k)) for k in far_first(n)]

    def direct_sum(axis, n, local, into):
        p = place[axis]
        copies = [send(local(around(p + k, n)), into.at[k - 1], to(axis, n, k)) for k in far_first(n)]
        return copies, into

    def together(*parts):
        last = [None] * len(parts)
        live = list(range(len(parts)))
        while live:
            for k in list(live):
                try:
                    last[k] = next(parts[k])
                except StopIteration:
                    live.remove(k)
        return last

    def gather_dp(buf):
        sibling = []

        def at(owner):
            return buf.at[2 * owner + core]

        def pass_on(owner):
            sibling.append(send(at(owner), at(owner), {"core": 1 - core}))

        def go(owner, step):
            return send(at(owner), at(owner), to("x", nx, step))

        ways = (sign, -sign)
        twos = [go(x, 2 * s) for s in ways]
        ones = [go(x, s) for s in ways]
        pass_on(x)
        threes = []
        for s, copy in zip(ways, twos):
            copy.wait_recv()
            owner = around(x - 2 * s, nx)
            if len(threes) == 0:
                four = go(owner, 2 * s)
            threes.append(go(owner, s))
        for s, copy in zip(ways, ones):
            copy.wait_recv()
            pass_on(around(x - s, nx))
        for s in ways:
            pass_on(around(x - 2 * s, nx))
        for s, copy in zip(ways, threes):
            copy.wait_recv()
            pass_on(around(x - 3 * s, nx))
        four.wait_recv()
        pass_on(around(x + 4, nx))
        for copy in sibling:
            copy.wait_recv()

    current = start_ref[...]
    for it in range(STEPS):
        matrix = current.astype(jnp.bfloat16)
        wide, mix, g = panel.at[it], mixed.at[it], gram.at[it]
        wide[dp] = matrix
        gather_dp(wide)

        sub = rows // SUBS
        turned = matrix.T

        def local_of(first, b):
            return lambda q: dot(turned[b * sub : (b + 1) * sub], wide[first + q])

        parts = [(h, b) for b in range(SUBS) for h in range(2)]
        sums = together(
            *(
                ring_sum(*half_of[h], local_of(h * nz, b), big_out.at[it, h, b], big_in.at[it, h, b], big_out.dtype)
                for h, b in parts
            )
        )
        part = rows // nz
        whole = held.at[it]
        for (h, b), value in zip(parts, sums):
            whole[h, b * sub : (b + 1) * sub] = value
            small_out[it, h, b * sub : (b + 1) * sub] = value.astype(SMALL)
        def part_of(h, of):
            return lambda q: of.at[h, pl.ds(pl.multiple_of(q * part, part), part), :]

        crossed = (half_of[1], half_of[0])
        started = [direct_sum(*crossed[h], part_of(h, small_out.at[it]), small_in.at[it, h]) for h in range(2)]
        own = (z, nz + y)

        def tile_of(h):
            return lambda q: g.at[own[h], pl.ds(pl.multiple_of(q * part, part), part), :]

        square = jnp.zeros((8, rows // 2), jnp.float32)
        arriving = []
        for h in range(2):
            axis, n = crossed[h]
            copies, into = started[h]
            value = part_of(h, whole)(place[axis])[...]
            for copy in copies:
                copy.wait_recv()
            tile = (value + jnp.sum(into[...].astype(jnp.float32), axis=0)).astype(jnp.bfloat16)
            tile_of(h)(place[axis])[...] = tile
            arriving += direct_gather(axis, n, tile_of(h))
            v = tile.astype(jnp.float32)
            v = (v * v).reshape(part // 8, 8, rows).sum(axis=0)
            square = square + v[:, : rows // 2] + v[:, rows // 2 :]
        told = []
        squares[it, 0, 0] = square
        for k in range(1, 2 * nx):
            other = lax.rem(dp + k, 2 * nx)
            told.append(send(squares.at[it, 0, 0], squares.at[it, 0, k], {"x": other // 2, "core": other % 2}))

        def spread(stage, axis, n):
            for copy in told:
                copy.wait_recv()
            count = 2 * nx if stage == 1 else n
            squares[it, stage, 0] = jnp.sum(squares[it, stage - 1, :count], axis=0)
            told[:] = [
                send(squares.at[it, stage, 0], squares.at[it, stage, k], to(axis, n, k)) for k in range(1, n)
            ]

        for copy in arriving:
            copy.wait_recv()

        first = []

        def use(block):
            first.append(dot(wide[block], g[block], (1, 1)))
            if len(first) > 1:
                first[:] = [first[0] + first[1]]

        rings = [
            ring_gather(
                *half_of[h],
                lambda o, h=h, b=b: g.at[h * nz + o, b * sub : (b + 1) * sub],
                lambda o, h=h, b=b: use(h * nz + o) if b == SUBS - 1 else None,
            )
            for h, b in parts
        ]
        for ring in rings:
            next(ring)
        use(own[0])
        use(own[1])
        spread(1, "z", nz)
        for ring in rings:
            next(ring)
        for ring in rings:
            next(ring)
        spread(2, "y", ny)
        together(*rings)
        for copy in told:
            copy.wait_recv()
        total = jnp.sum(squares[it, 2, :ny], axis=0)
        total = jnp.sum(jnp.sum(total, axis=1, keepdims=True), axis=0, keepdims=True)
        inverse_norm = lax.rsqrt(total)
        root_scale = jnp.sqrt(inverse_norm)
        matrix_full = matrix.astype(jnp.float32)
        mix[dp] = (
            cubic_term * root_scale * matrix_full + quintic_term * root_scale * inverse_norm * first[0]
        ).astype(jnp.bfloat16)
        gather_dp(mix)
        second = dot(mix[0], g[0], (1, 1))
        for j in range(1, 2 * nx):
            second = second + dot(mix[j], g[j], (1, 1))
        current = linear_term * root_scale * matrix_full + inverse_norm * second
    update_ref[...] = math.sqrt(D) * current
    for copy in sent:
        copy.wait_send()


def body(sizes, momentum, gradient):
    nx, nz, ny = sizes
    grad_full = gradient.T.astype(jnp.float32)
    new_momentum = momentum_decay * momentum.T + grad_full
    current = grad_full + momentum_decay * new_momentum
    columns, rows = current.shape
    part = rows // nz
    copies = STEPS * 150
    update = pl.pallas_call(
        lambda *refs: kernel(sizes, *refs),
        out_shape=jax.ShapeDtypeStruct((columns, rows), jnp.float32),
        in_specs=[pl.BlockSpec(memory_space=pltpu.VMEM)],
        out_specs=pl.BlockSpec(memory_space=pltpu.VMEM),
        scratch_shapes=[
            pltpu.VMEM((STEPS, 2 * nx, columns, rows), jnp.bfloat16),
            pltpu.VMEM((STEPS, 2 * nx, columns, rows), jnp.bfloat16),
            pltpu.VMEM((STEPS, nz + ny, rows, rows), jnp.bfloat16),
            pltpu.VMEM((STEPS, 2, SUBS, nz - 1, rows // SUBS, rows), SUM_TYPE),
            pltpu.VMEM((STEPS, 2, SUBS, nz - 1, rows // SUBS, rows), SUM_TYPE),
            pltpu.VMEM((STEPS, 2, rows, rows), jnp.float32),
            pltpu.VMEM((STEPS, 2, rows, rows), SMALL),
            pltpu.VMEM((STEPS, 2, nz - 1, part, rows), SMALL),
            pltpu.VMEM((STEPS, 3, 2 * nx, 8, rows // 2), jnp.float32),
            pltpu.SemaphoreType.DMA((copies,)),
            pltpu.SemaphoreType.DMA((copies,)),
        ],
        compiler_params=pltpu.CompilerParams(collective_id=0, has_side_effects=True, vmem_limit_bytes=52 * 2**20),
    )(current)
    return new_momentum.T, update.T


def solution(mesh):
    split = Mesh(mesh.devices.reshape(8, 2, 8, 8), ("x", "core", "z", "y"))
    spec = P(("x", "core"), ("z", "y"))
    return jax.shard_map(
        lambda m, g: body((8, 8, 8), m, g),
        mesh=split,
        in_specs=(spec, spec),
        out_specs=(spec, spec),
        check_vma=False,
    )
```

```python
import math

import jax
import jax.numpy as jnp
from jax import lax
from jax.experimental import pallas as pl
from jax.experimental.pallas import tpu as pltpu
from jax.sharding import Mesh
from jax.sharding import PartitionSpec as P

D = 7168
STEPS = 2
MESH = pl.DeviceIdType.MESH

momentum_decay = 0.95
linear_term = 3.4445
cubic_term = -4.775
quintic_term = 2.0315

SUM_TYPE = jnp.bfloat16
SMALL = jnp.bfloat16
SUBS = 2
SUM_SUBS = 4


def dot(a, b, dims=(1, 0)):
    return lax.dot_general(a, b, (((dims[0],), (dims[1],)), ((), ())), preferred_element_type=jnp.float32)


def kernel(sizes, start_ref, update_ref, panel, mixed, gram, big_out, big_in, held, small_out, small_in, squares, send_sem, recv_sem):
    nx, nz, ny = sizes
    half_of = (("z", nz), ("y", ny))
    x, core, z, y = (lax.axis_index(a) for a in ("x", "core", "z", "y"))
    place = {"x": x, "z": z, "y": y}
    dp = 2 * x + core
    sign = 1 - 2 * core
    rows = gram.shape[-1]

    def around(p, n):
        return lax.rem(p + 2 * n, n)

    def to(axis, n, step):
        return {axis: around(place[axis] + step, n)}

    barrier = pltpu.get_barrier_semaphore()
    for axis, n in half_of:
        for step in range(1, n):
            pl.semaphore_signal(barrier, inc=1, device_id=to(axis, n, step), device_id_type=MESH)
    for k in range(1, 2 * nx):
        other = lax.rem(dp + k, 2 * nx)
        pl.semaphore_signal(barrier, inc=1, device_id={"x": other // 2, "core": other % 2}, device_id_type=MESH)
    pl.semaphore_wait(barrier, nz + ny + 2 * nx - 3)

    sent = []

    def send(src, dst, device):
        k = len(sent)
        copy = pltpu.make_async_remote_copy(
            src_ref=src, dst_ref=dst, send_sem=send_sem.at[k], recv_sem=recv_sem.at[k], device_id=device, device_id_type=MESH
        )
        copy.start()
        sent.append(copy)
        return copy

    def ring_gather(axis, n, at, then):
        p = place[axis]
        ways = [[sign, n // 2, None], [-sign, (n - 1) // 2, None]]
        for t in range(n // 2 + 1):
            for way in ways:
                s, count, copy = way
                if t > count:
                    continue
                owner = around(p - s * t, n)
                if t > 0:
                    copy.wait_recv()
                if t < count:
                    way[2] = send(at(owner), at(owner), to(axis, n, s))
                if t > 0:
                    then(owner)
            yield

    def ring_sum(axis, n, local, out, into, add_type):
        p = place[axis]
        ways = [[sign, n // 2, None, 0], [-sign, (n - 1) // 2, None, n // 2]]
        for t in range(n // 2):
            for way in ways:
                s, count, copy, base = way
                if t >= count:
                    continue
                q = around(p + s * (count - t), n)
                value = local(q)
                if t > 0:
                    copy.wait_recv()
                    value = value + into[base + t - 1].astype(jnp.float32)
                out[base + t] = value.astype(add_type)
                way[2] = send(out.at[base + t], into.at[base + t], to(axis, n, s))
            yield
        value = local(p)
        for s, count, copy, base in ways:
            if count:
                copy.wait_recv()
                value = value + into[base + count - 1].astype(jnp.float32)
        yield value

    def far_first(n):
        return sorted(range(1, n), key=lambda k: -min(k, n - k))

    def direct_gather(axis, n, at):
        own = at(place[axis])
        return [send(own, own, to(axis, n, k)) for k in far_first(n)]

    def direct_sum(axis, n, local, into):
        p = place[axis]
        copies = [send(local(around(p + k, n)), into.at[k - 1], to(axis, n, k)) for k in far_first(n)]
        return copies, into

    def together(*parts):
        last = [None] * len(parts)
        live = list(range(len(parts)))
        while live:
            for k in list(live):
                try:
                    last[k] = next(parts[k])
                except StopIteration:
                    live.remove(k)
        return last

    def gather_dp(buf):
        sibling = []

        def at(owner):
            return buf.at[2 * owner + core]

        def pass_on(owner):
            sibling.append(send(at(owner), at(owner), {"core": 1 - core}))

        def go(owner, step):
            return send(at(owner), at(owner), to("x", nx, step))

        ways = (sign, -sign)
        twos = [go(x, 2 * s) for s in ways]
        ones = [go(x, s) for s in ways]
        pass_on(x)
        threes = []
        for s, copy in zip(ways, twos):
            copy.wait_recv()
            owner = around(x - 2 * s, nx)
            if len(threes) == 0:
                four = go(owner, 2 * s)
            threes.append(go(owner, s))
        for s, copy in zip(ways, ones):
            copy.wait_recv()
            pass_on(around(x - s, nx))
        for s in ways:
            pass_on(around(x - 2 * s, nx))
        for s, copy in zip(ways, threes):
            copy.wait_recv()
            pass_on(around(x - 3 * s, nx))
        four.wait_recv()
        pass_on(around(x + 4, nx))
        for copy in sibling:
            copy.wait_recv()

    current = start_ref[...]
    for it in range(STEPS):
        matrix = current.astype(jnp.bfloat16)
        wide, mix, g = panel.at[it], mixed.at[it], gram.at[it]
        wide[dp] = matrix
        gather_dp(wide)

        sub = rows // SUBS
        turned = matrix.T

        thin = rows // SUM_SUBS

        def local_of(first, b):
            return lambda q: dot(turned[b * thin : (b + 1) * thin], wide[first + q])

        parts = [(h, b) for b in range(SUBS) for h in range(2)]
        sum_parts = [(h, b) for b in range(SUM_SUBS) for h in range(2)]
        sums = together(
            *(
                ring_sum(*half_of[h], local_of(h * nz, b), big_out.at[it, h, b], big_in.at[it, h, b], big_out.dtype)
                for h, b in sum_parts
            )
        )
        part = rows // nz
        whole = held.at[it]
        for (h, b), value in zip(sum_parts, sums):
            whole[h, b * thin : (b + 1) * thin] = value
            small_out[it, h, b * thin : (b + 1) * thin] = value.astype(SMALL)
        def part_of(h, of):
            return lambda q: of.at[h, pl.ds(pl.multiple_of(q * part, part), part), :]

        crossed = (half_of[1], half_of[0])
        started = [direct_sum(*crossed[h], part_of(h, small_out.at[it]), small_in.at[it, h]) for h in range(2)]
        own = (z, nz + y)

        def tile_of(h):
            return lambda q: g.at[own[h], pl.ds(pl.multiple_of(q * part, part), part), :]

        square = jnp.zeros((8, rows // 2), jnp.float32)
        arriving = []
        for h in range(2):
            axis, n = crossed[h]
            copies, into = started[h]
            value = part_of(h, whole)(place[axis])[...]
            for copy in copies:
                copy.wait_recv()
            tile = (value + jnp.sum(into[...].astype(jnp.float32), axis=0)).astype(jnp.bfloat16)
            tile_of(h)(place[axis])[...] = tile
            arriving += direct_gather(axis, n, tile_of(h))
            v = tile.astype(jnp.float32)
            v = (v * v).reshape(part // 8, 8, rows).sum(axis=0)
            square = square + v[:, : rows // 2] + v[:, rows // 2 :]
        told = []
        squares[it, 0, 0] = square
        for k in range(1, 2 * nx):
            other = lax.rem(dp + k, 2 * nx)
            told.append(send(squares.at[it, 0, 0], squares.at[it, 0, k], {"x": other // 2, "core": other % 2}))

        def spread(stage, axis, n):
            for copy in told:
                copy.wait_recv()
            count = 2 * nx if stage == 1 else n
            squares[it, stage, 0] = jnp.sum(squares[it, stage - 1, :count], axis=0)
            told[:] = [
                send(squares.at[it, stage, 0], squares.at[it, stage, k], to(axis, n, k)) for k in range(1, n)
            ]

        for copy in arriving:
            copy.wait_recv()

        first = []

        def use(block):
            first.append(dot(wide[block], g[block], (1, 1)))
            if len(first) > 1:
                first[:] = [first[0] + first[1]]

        rings = [
            ring_gather(
                *half_of[h],
                lambda o, h=h, b=b: g.at[h * nz + o, b * sub : (b + 1) * sub],
                lambda o, h=h, b=b: use(h * nz + o) if b == SUBS - 1 else None,
            )
            for h, b in parts
        ]
        for ring in rings:
            next(ring)
        use(own[0])
        use(own[1])
        spread(1, "z", nz)
        for ring in rings:
            next(ring)
        for ring in rings:
            next(ring)
        spread(2, "y", ny)
        together(*rings)
        for copy in told:
            copy.wait_recv()
        total = jnp.sum(squares[it, 2, :ny], axis=0)
        total = jnp.sum(jnp.sum(total, axis=1, keepdims=True), axis=0, keepdims=True)
        inverse_norm = lax.rsqrt(total)
        root_scale = jnp.sqrt(inverse_norm)
        matrix_full = matrix.astype(jnp.float32)
        mix[dp] = (
            cubic_term * root_scale * matrix_full + quintic_term * root_scale * inverse_norm * first[0]
        ).astype(jnp.bfloat16)
        gather_dp(mix)
        second = dot(mix[0], g[0], (1, 1))
        for j in range(1, 2 * nx):
            second = second + dot(mix[j], g[j], (1, 1))
        current = linear_term * root_scale * matrix_full + inverse_norm * second
    update_ref[...] = math.sqrt(D) * current
    for copy in sent:
        copy.wait_send()


def body(sizes, momentum, gradient):
    nx, nz, ny = sizes
    grad_full = gradient.T.astype(jnp.float32)
    new_momentum = momentum_decay * momentum.T + grad_full
    current = grad_full + momentum_decay * new_momentum
    columns, rows = current.shape
    part = rows // nz
    copies = STEPS * 175
    update = pl.pallas_call(
        lambda *refs: kernel(sizes, *refs),
        out_shape=jax.ShapeDtypeStruct((columns, rows), jnp.float32),
        in_specs=[pl.BlockSpec(memory_space=pltpu.VMEM)],
        out_specs=pl.BlockSpec(memory_space=pltpu.VMEM),
        scratch_shapes=[
            pltpu.VMEM((STEPS, 2 * nx, columns, rows), jnp.bfloat16),
            pltpu.VMEM((STEPS, 2 * nx, columns, rows), jnp.bfloat16),
            pltpu.VMEM((STEPS, nz + ny, rows, rows), jnp.bfloat16),
            pltpu.VMEM((STEPS, 2, SUM_SUBS, nz - 1, rows // SUM_SUBS, rows), SUM_TYPE),
            pltpu.VMEM((STEPS, 2, SUM_SUBS, nz - 1, rows // SUM_SUBS, rows), SUM_TYPE),
            pltpu.VMEM((STEPS, 2, rows, rows), jnp.float32),
            pltpu.VMEM((STEPS, 2, rows, rows), SMALL),
            pltpu.VMEM((STEPS, 2, nz - 1, part, rows), SMALL),
            pltpu.VMEM((STEPS, 3, 2 * nx, 8, rows // 2), jnp.float32),
            pltpu.SemaphoreType.DMA((copies,)),
            pltpu.SemaphoreType.DMA((copies,)),
        ],
        compiler_params=pltpu.CompilerParams(collective_id=0, has_side_effects=True, vmem_limit_bytes=52 * 2**20),
    )(current)
    return new_momentum.T, update.T


def solution(mesh):
    split = Mesh(mesh.devices.reshape(8, 2, 8, 8), ("x", "core", "z", "y"))
    spec = P(("x", "core"), ("z", "y"))
    return jax.shard_map(
        lambda m, g: body((8, 8, 8), m, g),
        mesh=split,
        in_specs=(spec, spec),
        out_specs=(spec, spec),
        check_vma=False,
    )
```
